32 devices in a mesh: img: 16 (over z, x, core), tok: 2 (over y).
Axes of the slice: x: 2, y: 2, z: 4, core: 2. Of those that a mesh axis runs over, the one named last changes fastest.
Arguments:
- tokens: bfloat16 [16, 2064, 1024], P('img', 'tok'), may hold values from -6 to 6
- block_lengths: int32 [16, 2], P('img'), may hold values from 64 to 1032, as said below
- out_grad: bfloat16 [16, 2064, 1024], P('img', 'tok'), may hold values from -6 to 6
- qkv_weight: float32 [1024, 3072], P(('img', 'tok')), may hold values from -0.1875 to 0.1875
- proj_weight: float32 [1024, 1024], P(('img', 'tok')), may hold values from -3.5 to 3.5
- up_weight: float32 [1024, 4096], P(('img', 'tok')), may hold values from -0.1875 to 0.1875
- down_weight: float32 [4096, 1024], P(('img', 'tok')), may hold values from -0.1875 to 0.1875
- gain_rows: float32 [4, 1024], P(None, ('img', 'tok')), may hold values from 0.25 to 1.75
- bias_rows: float32 [10, 1024], P(None, ('img', 'tok')), may hold values from -3 to 3
- qkv_first: float32 [1024, 3072], P(('img', 'tok')), may hold values from -96 to 96
- proj_first: float32 [1024, 1024], P(('img', 'tok')), may hold values from -5 to 5
- up_first: float32 [1024, 4096], P(('img', 'tok')), may hold values from -96 to 96
- down_first: float32 [4096, 1024], P(('img', 'tok')), may hold values from -56 to 56
- gain_first: float32 [4, 1024], P(None, ('img', 'tok')), may hold values from -192 to 192
- bias_first: float32 [10, 1024], P(None, ('img', 'tok')), may hold values from -96 to 96
- qkv_second: float32 [1024, 3072], P(('img', 'tok')), may hold values from 21.92 to 87.68
- proj_second: float32 [1024, 1024], P(('img', 'tok')), may hold values from 0.0548 to 0.2192
- up_second: float32 [1024, 4096], P(('img', 'tok')), may hold values from 21.92 to 87.68
- down_second: float32 [4096, 1024], P(('img', 'tok')), may hold values from 7.8912 to 31.5648
- gain_second: float32 [4, 1024], P(None, ('img', 'tok')), may hold values from 43.84 to 175.36
- bias_second: float32 [10, 1024], P(None, ('img', 'tok')), may hold values from 21.92 to 87.68
Outputs:
- output: bfloat16 [16, 2064, 1024], P('img', 'tok')
- input_grad: bfloat16 [16, 2064, 1024], P('img', 'tok')
- qkv_first_new: float32 [1024, 3072], P(('img', 'tok'))
- proj_first_new: float32 [1024, 1024], P(('img', 'tok'))
- up_first_new: float32 [1024, 4096], P(('img', 'tok'))
- down_first_new: float32 [4096, 1024], P(('img', 'tok'))
- gain_first_new: float32 [4, 1024], P(None, ('img', 'tok'))
- bias_first_new: float32 [10, 1024], P(None, ('img', 'tok'))
- qkv_second_new: float32 [1024, 3072], P(('img', 'tok'))
- proj_second_new: float32 [1024, 1024], P(('img', 'tok'))
- up_second_new: float32 [1024, 4096], P(('img', 'tok'))
- down_second_new: float32 [4096, 1024], P(('img', 'tok'))
- gain_second_new: float32 [4, 1024], P(None, ('img', 'tok'))
- bias_second_new: float32 [10, 1024], P(None, ('img', 'tok'))
- qkv_new: float32 [1024, 3072], P(('img', 'tok'))
- proj_new: float32 [1024, 1024], P(('img', 'tok'))
- up_new: float32 [1024, 4096], P(('img', 'tok'))
- down_new: float32 [4096, 1024], P(('img', 'tok'))
- gain_new: float32 [4, 1024], P(None, ('img', 'tok'))
- bias_new: float32 [10, 1024], P(None, ('img', 'tok'))
The draws below stay inside these ranges and needn't reach their ends.
Inputs may be any that keep to these rules, and one draw needn't show every extreme that they name: `block_lengths`: for each image the blocks sum to 1370, each holds 64 or more, and one block of every image holds exactly 1032.
All inputs are finite; a program needn't handle non-finite values.
Results may differ from the reference program's by a relative error of at most 0.013.
The reference program's roundings to bfloat16 on the way count: a program that leaves them out, or rounds other values in their place, can miss the bound.
Values may be sent and summed in bfloat16 or wider, within the bound.
A program may use at most 320 MiB of HBM per device.

```python
import math
import jax
import jax.numpy as jnp
from jax import lax

D = 1024
H = 16
HD = 64
FF = 4096
LEN = 1370
LOW = 64
STEP = 10
CAP = 1032
IMAGES = 16
NBIAS = 10
N_TOK = 2


def draw_block_lengths(key, part):
    key = jax.random.fold_in(key, 11)
    key_widest, key_weights = jax.random.split(key)
    widest = jax.random.randint(key_widest, (IMAGES,), 0, N_TOK)
    weights_int = jax.random.randint(key_weights, (IMAGES, N_TOK), 2, 4)
    is_widest = jnp.arange(N_TOK)[None, :] == widest[:, None]
    weights_int = jnp.where(is_widest, 0, weights_int)
    weight_total = jnp.sum(weights_int, axis=1, keepdims=True)
    remaining = LEN - CAP - (N_TOK - 1) * LOW
    shares = remaining * weights_int // weight_total
    leftover = remaining - jnp.sum(shares, axis=1, keepdims=True)
    ranking = jnp.cumsum(jnp.where(is_widest, 0, 1), axis=1) - 1
    extra_one = jnp.where(jnp.logical_and(jnp.logical_not(is_widest), ranking < leftover), 1, 0)
    lengths_out = jnp.where(is_widest, CAP, LOW + shares + extra_one)
    return lengths_out.astype(jnp.int32)


def draw_bias_rows(key, part):
    key = jax.random.fold_in(key, 12)
    sampled = 0.5 * jax.random.truncated_normal(key, -6.0, 6.0, (NBIAS, D), jnp.float32)
    value_scale = ((3 * D // LEN + 1) / D) ** 0.5
    row_scale = jnp.where(jnp.arange(NBIAS)[:, None] == 2, value_scale, 1.0)
    return (sampled * row_scale).astype(jnp.float32)


def levels(key, extent, cuts, low, top_value):
    def one(dim, shards_of):
        heights = jax.random.uniform(jax.random.fold_in(jax.random.fold_in(key, 6), dim), (shards_of,), jnp.float32, low / len(cuts), top_value / len(cuts))
        return jnp.repeat(jnp.exp(heights), extent[dim] // shards_of).reshape((-1,) + (1,) * (len(extent) - dim - 1))

    factor_of = one(*cuts[0])
    for cut in cuts[1:]:
        factor_of = factor_of * one(*cut)
    return factor_of


def noise(own_key, extent, deviation, most, cuts=(), held_as=jnp.bfloat16):
    factor_of = levels(own_key, extent, cuts, -0.22, 0.18) if cuts else 1.0
    values = jax.random.normal(own_key, extent, jnp.float32) * deviation * factor_of
    return jnp.minimum(jnp.maximum(values, -most), most).astype(held_as)


def setup_inputs(seed: int = 0) -> dict:
    splits = jax.random.split(jax.random.key(seed), 22)
    return {
        "tokens": noise(splits[0], (IMAGES, N_TOK * CAP, D), 1.0, 6.0, ((0, 16), (1, 2))),
        "block_lengths": draw_block_lengths(jax.random.fold_in(splits[21], 71), 0),
        "out_grad": noise(splits[2], (IMAGES, N_TOK * CAP, D), 1.0, 6.0, ((0, 16), (1, 2))),
        "qkv_weight": noise(splits[3], (D, 3 * D), D ** -0.5, 0.1875, ((0, 32),), jnp.float32),
        "proj_weight": noise(splits[4], (D, D), (3 * D // LEN + 1) ** -0.5, 3.5, ((0, 32),), jnp.float32),
        "up_weight": noise(splits[5], (D, FF), D ** -0.5, 0.1875, ((0, 32),), jnp.float32),
        "down_weight": noise(splits[6], (FF, D), (FF // 4) ** -0.5, 0.1875, ((0, 32),), jnp.float32),
        "gain_rows": jnp.clip(1.0 + 0.15 * jax.random.normal(splits[7], (4, D), jnp.float32), 0.25, 1.75),
        "bias_rows": draw_bias_rows(jax.random.fold_in(splits[21], 71), 0),
        "qkv_first": noise(splits[9], (D, 3 * D), (0.11 * (IMAGES * LEN) ** 0.5), 96.0, ((0, 32),), jnp.float32),
        "proj_first": noise(splits[10], (D, D), (0.0055 * (IMAGES * LEN) ** 0.5), 5.0, ((0, 32),), jnp.float32),
        "up_first": noise(splits[11], (D, FF), (0.11 * (IMAGES * LEN) ** 0.5), 96.0, ((0, 32),), jnp.float32),
        "down_first": noise(splits[12], (FF, D), (0.066 * (IMAGES * LEN) ** 0.5), 56.0, ((0, 32),), jnp.float32),
        "gain_first": noise(splits[13], (4, D), (0.2 * (IMAGES * LEN) ** 0.5), 192.0, ((1, 32),), jnp.float32),
        "bias_first": noise(splits[14], (NBIAS, D), (0.11 * (IMAGES * LEN) ** 0.5), 96.0, ((1, 32),), jnp.float32),
        "qkv_second": jnp.clip(jnp.exp(math.log(87.68) - 1.3862944 * jax.random.uniform(splits[15], (D, 3 * D), jnp.float32) ** levels(splits[15], (D, 3 * D), ((0, 32),), -0.2, 0.2)), 21.92, 87.68),
        "proj_second": jnp.clip(jnp.exp(math.log(0.2192) - 1.3862944 * jax.random.uniform(splits[16], (D, D), jnp.float32) ** levels(splits[16], (D, D), ((0, 32),), -0.2, 0.2)), 0.0548, 0.2192),
        "up_second": jnp.clip(jnp.exp(math.log(87.68) - 1.3862944 * jax.random.uniform(splits[17], (D, FF), jnp.float32) ** levels(splits[17], (D, FF), ((0, 32),), -0.2, 0.2)), 21.92, 87.68),
        "down_second": jnp.clip(jnp.exp(math.log(31.5648) - 1.3862944 * jax.random.uniform(splits[18], (FF, D), jnp.float32) ** levels(splits[18], (FF, D), ((0, 32),), -0.2, 0.2)), 7.8912, 31.5648),
        "gain_second": jnp.clip(jnp.exp(math.log(175.36) - 1.3862944 * jax.random.uniform(splits[19], (4, D), jnp.float32) ** levels(splits[19], (4, D), ((1, 32),), -0.2, 0.2)), 43.84, 175.36),
        "bias_second": jnp.clip(jnp.exp(math.log(87.68) - 1.3862944 * jax.random.uniform(splits[20], (NBIAS, D), jnp.float32) ** levels(splits[20], (NBIAS, D), ((1, 32),), -0.2, 0.2)), 21.92, 87.68),
    }


@jax.custom_vjp
def low(v):
    return lax.optimization_barrier(v.astype(jnp.bfloat16)).astype(jnp.float32)

@jax.custom_vjp
def low_back(v):
    return v

def low_keep(v):
    return (low(v), None)

def low_pass(kept, grad):
    return (grad,)

def back_keep(v):
    return (v, None)

def back_low(kept, grad):
    return (low(grad),)
low.defvjp(low_keep, low_pass)
low_back.defvjp(back_keep, back_low)
norm_eps = 1e-06
beta_one = 0.9
beta_two = 0.999
adam_eps = 1e-08
learn_rates = (0.1, 1.5, 0.1, 0.05, 0.5, 0.5)
decay_rates = (0.05, 0.05, 0.05, 0.05, 0.0, 0.0)

def exact_dot(operand, matrix):
    return jnp.dot(operand, matrix, precision=lax.Precision.HIGHEST, preferred_element_type=jnp.float32)

def norm_rows(values, scales, shifts):
    centred = values - lax.optimization_barrier(jnp.mean(values, axis=-1, keepdims=True))
    spread = lax.optimization_barrier(jnp.mean(centred * centred, axis=-1, keepdims=True))
    return centred * lax.rsqrt(spread + norm_eps) * scales + shifts

def attend(queries, keyset, valset, key_valid):
    length = queries.shape[0]
    query_blocks = queries.reshape(N_TOK, CAP, H, HD)
    keys_heads = keyset.reshape(length, H, HD)
    vals_heads = valset.reshape(length, H, HD)

    def one_block(query_block):
        scores = jnp.einsum('qhd,khd->hqk', query_block, keys_heads, precision=lax.Precision.HIGHEST, preferred_element_type=jnp.float32)
        scores = low_back(jnp.where(key_valid[None, None, :], scores, -1e+30))
        attn_weight = low(jax.nn.softmax(scores, axis=-1))
        mixed_out = jnp.einsum('hqk,khd->qhd', attn_weight, vals_heads, precision=lax.Precision.HIGHEST, preferred_element_type=jnp.float32)
        return mixed_out.reshape(CAP, H * HD)
    return lax.map(jax.checkpoint(one_block), query_blocks).reshape(length, H * HD)

def layer(values, row_valid, key_valid, qkv_weight, proj_weight, up_weight, down_weight, gain_rows, bias_rows):
    width = values.shape[1]
    normed = low(norm_rows(values, gain_rows[0], bias_rows[0]))
    mixed_qkv = exact_dot(normed, qkv_weight)
    queries = low(low_back((mixed_qkv[:, :width] + bias_rows[1]) * HD ** (-0.5)))
    keyset = low(low_back(mixed_qkv[:, width:2 * width]))
    valset = low(low_back(mixed_qkv[:, 2 * width:] + bias_rows[2]))
    attended = low(low_back(attend(queries, keyset, valset, key_valid)))
    branch = low_back(exact_dot(attended, proj_weight) + bias_rows[3])
    middle = values + gain_rows[1] * branch
    normed_two = low(norm_rows(middle, gain_rows[2], bias_rows[4]))
    hidden_pre = low_back(exact_dot(normed_two, up_weight) + bias_rows[6:].reshape(-1))
    hidden = low(jax.nn.gelu(hidden_pre, approximate=False))
    second = low_back(exact_dot(hidden, down_weight) + bias_rows[5])
    result = middle + gain_rows[3] * second
    return result * row_valid[:, None]

def adam_update(weight, gradient, first, second, rate, decay):
    first_new = beta_one * first + (1.0 - beta_one) * gradient
    second_new = beta_two * second + (1.0 - beta_two) * gradient * gradient
    corrected = first_new / (1.0 - beta_one ** STEP)
    scaled = second_new / (1.0 - beta_two ** STEP)
    weight_new = weight - rate * (corrected / (jnp.sqrt(scaled) + adam_eps) + decay * weight)
    return (first_new, second_new, weight_new)

def reference(tokens, block_lengths, out_grad, qkv_weight, proj_weight, up_weight, down_weight, gain_rows, bias_rows, qkv_first, proj_first, up_first, down_first, gain_first, bias_first, qkv_second, proj_second, up_second, down_second, gain_second, bias_second):
    params = (qkv_weight, proj_weight, up_weight, down_weight, gain_rows, bias_rows)
    firsts = (qkv_first, proj_first, up_first, down_first, gain_first, bias_first)
    seconds = (qkv_second, proj_second, up_second, down_second, gain_second, bias_second)
    rounded = tuple((low(param) for param in params))
    positions = jnp.arange(CAP, dtype=jnp.int32)

    def per_image(running, inputs):
        image_tokens, image_grad, image_lengths = inputs
        row_ok = (positions[None, :] < image_lengths[:, None]).reshape(-1)
        row_valid = row_ok.astype(jnp.float32)

        def forward(values, *weights_all):
            return layer(values, row_valid, row_ok, *weights_all)
        result, pullback = jax.vjp(forward, image_tokens.astype(jnp.float32), *rounded)
        gradients = pullback(image_grad.astype(jnp.float32))
        running = tuple((summed + gradient for summed, gradient in zip(running, gradients[1:])))
        return (running, (result.astype(jnp.bfloat16), gradients[0].astype(jnp.bfloat16)))
    zeros_start = tuple((jnp.zeros(param.shape, jnp.float32) for param in params))
    totals, outputs = lax.scan(per_image, zeros_start, (tokens, out_grad, block_lengths))
    output, input_grad = outputs
    updated = [adam_update(params[position], totals[position], firsts[position], seconds[position], learn_rates[position], decay_rates[position]) for position in range(6)]
    return (output, input_grad, updated[0][0], updated[1][0], updated[2][0], updated[3][0], updated[4][0], updated[5][0], updated[0][1], updated[1][1], updated[2][1], updated[3][1], updated[4][1], updated[5][1], updated[0][2], updated[1][2], updated[2][2], updated[3][2], updated[4][2], updated[5][2])
```

```python
from functools import partial

import jax
import jax.numpy as jnp
from jax import lax
from jax.experimental import pallas as pl
from jax.experimental.pallas import tpu as pltpu
from jax.sharding import PartitionSpec as P

HD = 64
STEP = 10
LEN = 1370
LANES = 128
QUERY_BLOCK = 256
VMEM_BYTES = 28 * 1024 * 1024


norm_eps = 1e-06
beta_one = 0.9
beta_two = 0.999
adam_eps = 1e-08
learn_rates = (0.1, 1.5, 0.1, 0.05, 0.5, 0.5)
decay_rates = (0.05, 0.05, 0.05, 0.05, 0.0, 0.0)


def norm_rows(values, scales, shifts):
    centred = values - jnp.mean(values, axis=-1, keepdims=True)
    spread = jnp.mean(centred * centred, axis=-1, keepdims=True)
    return centred * lax.rsqrt(spread + norm_eps) * scales + shifts


def adam_update(weight, gradient, first, second, rate, decay):
    first_new = beta_one * first + (1.0 - beta_one) * gradient
    second_new = beta_two * second + (1.0 - beta_two) * gradient * gradient
    corrected = first_new / (1.0 - beta_one**STEP)
    scaled = second_new / (1.0 - beta_two**STEP)
    weight_new = weight - rate * (corrected / (jnp.sqrt(scaled) + adam_eps) + decay * weight)
    return (first_new, second_new, weight_new)


def lane_head(shape, head):
    lane = lax.broadcasted_iota(jnp.int32, shape, 1)
    return jnp.logical_and(lane >= head * HD, lane < (head + 1) * HD)


def live_rows(ref, row_count):
    block = ref[...]
    first = pl.program_id(1) * block.shape[0]
    row = first + lax.broadcasted_iota(jnp.int32, block.shape, 0)
    return jnp.where(row < row_count, block, jnp.zeros_like(block))


def scores_by_key(key_pair, query_pair, valid, head):
    query = jnp.where(lane_head(query_pair.shape, head), query_pair, jnp.zeros_like(query_pair))
    scores = lax.dot_general(
        key_pair, query, (((1,), (1,)), ((), ())), preferred_element_type=jnp.float32
    )
    return jnp.where(valid > 0.5, scores, -1e30)


def attend_kernel(row_count, q_ref, k_ref, v_ref, valid_ref, out_ref, log_ref):
    query_pair = live_rows(q_ref, row_count)
    key_pair = k_ref[...]
    value_by_lane = v_ref[...].T
    valid = valid_ref[...]
    parts = []
    for head in range(LANES // HD):
        scores = scores_by_key(key_pair, query_pair, valid, head)
        highest = jnp.max(scores, axis=0, keepdims=True)
        exponent = jnp.exp(scores - highest)
        totals = jnp.sum(exponent, axis=0, keepdims=True)
        attn = (exponent * (1.0 / totals)).astype(jnp.bfloat16)
        parts.append(
            jnp.dot(
                value_by_lane[head * HD : (head + 1) * HD], attn, preferred_element_type=jnp.float32
            )
        )
        log_ref[0, head : head + 1, :] = highest + jnp.log(totals)
    out_ref[...] = jnp.concatenate(parts, axis=0).T.astype(out_ref.dtype)


def back_kernel(
    row_count, q_ref, k_ref, v_ref, g_ref, log_ref, valid_ref, dq_ref, dk_ref, dv_ref
):
    @pl.when(pl.program_id(1) == 0)
    def _():
        dk_ref[...] = jnp.zeros_like(dk_ref)
        dv_ref[...] = jnp.zeros_like(dv_ref)

    query_pair = live_rows(q_ref, row_count)
    grad_pair = live_rows(g_ref, row_count)
    key_pair = k_ref[...]
    value_pair = v_ref[...]
    key_by_lane = key_pair.T
    valid = valid_ref[...]
    parts = []
    for head in range(LANES // HD):
        own = lane_head(query_pair.shape, head)
        query = jnp.where(own, query_pair, jnp.zeros_like(query_pair))
        grad = jnp.where(own, grad_pair, jnp.zeros_like(grad_pair))
        scores = scores_by_key(key_pair, query_pair, valid, head)
        attn = jnp.exp(scores - log_ref[0, head : head + 1, :])
        grad_attn = lax.dot_general(
            value_pair, grad, (((1,), (1,)), ((), ())), preferred_element_type=jnp.float32
        )
        inner = jnp.sum(attn * grad_attn, axis=0, keepdims=True)
        grad_scores = (attn * (grad_attn - inner)).astype(jnp.bfloat16)
        dv_ref[...] += jnp.dot(
            attn.astype(jnp.bfloat16), grad, preferred_element_type=jnp.float32
        )
        dk_ref[...] += jnp.dot(grad_scores, query, preferred_element_type=jnp.float32)
        parts.append(
            jnp.dot(
                key_by_lane[head * HD : (head + 1) * HD],
                grad_scores,
                preferred_element_type=jnp.float32,
            )
        )
    dq_ref[...] = jnp.concatenate(parts, axis=0).T.astype(dq_ref.dtype)


def attention_specs(row_count, key_count, width):
    block = min(QUERY_BLOCK, row_count)
    blocks = -(-row_count // block)
    pairs = width // LANES
    rows = pl.BlockSpec((block, LANES), lambda p, i: (i, p))
    keys = pl.BlockSpec((key_count, LANES), lambda p, i: (0, p))
    logs = pl.BlockSpec((1, LANES // HD, block), lambda p, i: (p, 0, i))
    valid = pl.BlockSpec((key_count, 1), lambda p, i: (0, 0))
    return (block, blocks, pairs, rows, keys, logs, valid)


def attend(queries, keys, values, valid):
    row_count, width = queries.shape
    key_count = keys.shape[0]
    block, blocks, pairs, rows, keyed, logs, valid_spec = attention_specs(
        row_count, key_count, width
    )
    work = row_count * key_count * width
    return pl.pallas_call(
        partial(attend_kernel, row_count),
        grid=(pairs, blocks),
        in_specs=[rows, keyed, keyed, valid_spec],
        out_specs=[rows, logs],
        out_shape=[
            jax.ShapeDtypeStruct((row_count, width), jnp.bfloat16),
            jax.ShapeDtypeStruct((pairs, LANES // HD, blocks * block), jnp.float32),
        ],
        compiler_params=pltpu.CompilerParams(vmem_limit_bytes=VMEM_BYTES),
        cost_estimate=pl.CostEstimate(
            flops=16 * work, bytes_accessed=4 * key_count * width, transcendentals=work // HD
        ),
        name="attend",
    )(queries, keys, values, valid)


def attend_back(queries, keys, values, grads, logs_in, valid):
    row_count, width = queries.shape
    key_count = keys.shape[0]
    block, blocks, pairs, rows, keyed, logs, valid_spec = attention_specs(
        row_count, key_count, width
    )
    work = row_count * key_count * width
    return pl.pallas_call(
        partial(back_kernel, row_count),
        grid=(pairs, blocks),
        in_specs=[rows, keyed, keyed, rows, logs, valid_spec],
        out_specs=[rows, keyed, keyed],
        out_shape=[
            jax.ShapeDtypeStruct((row_count, width), jnp.bfloat16),
            jax.ShapeDtypeStruct((key_count, width), jnp.float32),
            jax.ShapeDtypeStruct((key_count, width), jnp.float32),
        ],
        compiler_params=pltpu.CompilerParams(vmem_limit_bytes=VMEM_BYTES),
        cost_estimate=pl.CostEstimate(
            flops=40 * work, bytes_accessed=12 * key_count * width, transcendentals=work // HD
        ),
        name="attend_back",
    )(queries, keys, values, grads, logs_in, valid)


def reduce_rows(gradient):
    return lax.psum_scatter(
        gradient, ("img", "tok"), scatter_dimension=0, tiled=True
    ).astype(jnp.float32)


def per_device(
    tokens,
    block_lengths,
    out_grad,
    qkv_weight,
    proj_weight,
    up_weight,
    down_weight,
    gain_rows,
    bias_rows,
    qkv_first,
    proj_first,
    up_first,
    down_first,
    gain_first,
    bias_first,
    qkv_second,
    proj_second,
    up_second,
    down_second,
    gain_second,
    bias_second,
):
    capacity, width = tokens.shape[1:]
    tok_count = lax.axis_size("tok")
    tok_here = lax.axis_index("tok")
    w_qkv = lax.all_gather(qkv_weight.astype(jnp.bfloat16), ("img", "tok"), axis=0, tiled=True)
    rows_all = lax.all_gather(
        jnp.concatenate([gain_rows, bias_rows], axis=0).astype(jnp.bfloat16),
        ("img", "tok"),
        axis=1,
        tiled=True,
    ).astype(jnp.float32)
    w_proj = lax.all_gather(proj_weight.astype(jnp.bfloat16), ("img", "tok"), axis=0, tiled=True)
    w_up = lax.all_gather(up_weight.astype(jnp.bfloat16), ("img", "tok"), axis=0, tiled=True)
    w_down = lax.all_gather(down_weight.astype(jnp.bfloat16), ("img", "tok"), axis=0, tiled=True)
    gain_count = gain_rows.shape[0]
    gain_all = rows_all[:gain_count]
    bias_all = rows_all[gain_count:]
    hidden_width = w_up.shape[1]
    query_scale = HD ** (-0.5)
    lengths = block_lengths[0]
    own_length = lengths[tok_here]
    short = -(-(LEN - capacity) // 8) * 8
    balanced = tok_count == 2 and capacity > short and (capacity - short) % 16 == 0
    swap = [(0, 1), (1, 0)]
    is_full = own_length > short
    if balanced:
        row_count = (capacity + short) // 2
        moved = row_count - short

        def take_rows(block):
            received = lax.ppermute(block[row_count:], "tok", swap)
            kept = jnp.where(is_full, block[short:row_count], received)
            return jnp.concatenate([block[:short], kept], axis=0)

        def give_rows(block):
            received = lax.ppermute(block[short:], "tok", swap)
            kept = jnp.where(is_full, block[short:], 0)
            tail = jnp.where(is_full, received, 0)
            return jnp.concatenate([block[:short], kept, tail], axis=0)

        def live_of(length):
            row = jnp.arange(row_count)
            return jnp.logical_or(row < length, row >= short)

    else:
        row_count = capacity

        def take_rows(block):
            return block

        def give_rows(block):
            return block

        def live_of(length):
            return jnp.arange(row_count) < length

    row_valid = live_of(own_length).astype(jnp.float32)[:, None]
    if tok_count == 2:
        key_valid = jnp.concatenate([live_of(own_length), live_of(lengths[1 - tok_here])])

        def gather_rows(block):
            return jnp.concatenate([block, lax.ppermute(block, "tok", swap)], axis=0)

        def scatter_rows(block):
            received = lax.ppermute(block[row_count:].astype(jnp.bfloat16), "tok", swap)
            return (block[:row_count] + received.astype(jnp.float32)).astype(jnp.bfloat16)

    else:
        key_valid = jnp.concatenate([live_of(lengths[place]) for place in range(tok_count)])

        def gather_rows(block):
            return lax.all_gather(block, "tok", axis=0, tiled=True)

        def scatter_rows(block):
            return lax.psum_scatter(
                block.astype(jnp.bfloat16), "tok", scatter_dimension=0, tiled=True
            )

    key_valid = key_valid.astype(jnp.float32)[:, None]
    values = take_rows(tokens[0]).astype(jnp.float32)
    normed = norm_rows(values, gain_all[0], bias_all[0]).astype(jnp.bfloat16)
    keyset = jnp.dot(
        normed, w_qkv[:, width : 2 * width], preferred_element_type=jnp.float32
    ).astype(jnp.bfloat16)
    valset = (
        jnp.dot(normed, w_qkv[:, 2 * width :], preferred_element_type=jnp.float32) + bias_all[2]
    ).astype(jnp.bfloat16)
    key_all = gather_rows(keyset)
    value_all = gather_rows(valset)
    queries = (
        (jnp.dot(normed, w_qkv[:, :width], preferred_element_type=jnp.float32) + bias_all[1])
        * query_scale
    ).astype(jnp.bfloat16)
    attended, log_totals = attend(queries, key_all, value_all, key_valid)
    branch = jnp.dot(attended, w_proj, preferred_element_type=jnp.float32) + bias_all[3]
    middle = values + gain_all[1] * branch
    normed_two = norm_rows(middle, gain_all[2], bias_all[4]).astype(jnp.bfloat16)
    hidden_pre = jnp.dot(normed_two, w_up, preferred_element_type=jnp.float32) + bias_all[
        6:
    ].reshape(hidden_width)
    hidden = jax.nn.gelu(hidden_pre, approximate=False).astype(jnp.bfloat16)
    second = jnp.dot(hidden, w_down, preferred_element_type=jnp.float32) + bias_all[5]
    result = middle + gain_all[3] * second
    output = give_rows((result * row_valid).astype(jnp.bfloat16))[None]
    grad_out = take_rows(out_grad[0]).astype(jnp.float32) * row_valid
    grad_second = (gain_all[3] * grad_out).astype(jnp.bfloat16)
    grad_gain_three = jnp.sum(grad_out * second, axis=0)
    grad_bias_down = jnp.sum(grad_second.astype(jnp.float32), axis=0)
    grad_down = jnp.einsum(
        "rf,rd->fd", hidden, grad_second, preferred_element_type=jnp.float32
    ).astype(jnp.bfloat16)
    grad_down, w_down = lax.optimization_barrier((grad_down, w_down))
    sum_down = reduce_rows(grad_down)
    grad_hidden = jnp.einsum("rd,fd->rf", grad_second, w_down, preferred_element_type=jnp.float32)
    _, gelu_pull = jax.vjp(partial(jax.nn.gelu, approximate=False), hidden_pre)
    grad_hidden_pre = gelu_pull(grad_hidden)[0].astype(jnp.bfloat16)
    grad_bias_up = jnp.sum(grad_hidden_pre.astype(jnp.float32), axis=0).reshape(
        hidden_width // width, width
    )
    grad_up = jnp.einsum(
        "rd,rf->df", normed_two, grad_hidden_pre, preferred_element_type=jnp.float32
    ).astype(jnp.bfloat16)
    grad_up, grad_hidden_pre = lax.optimization_barrier((grad_up, grad_hidden_pre))
    grad_normed_two = jnp.einsum(
        "rf,df->rd", grad_hidden_pre, w_up, preferred_element_type=jnp.float32
    )
    _, norm_two_pull = jax.vjp(norm_rows, middle, gain_all[2], bias_all[4])
    grad_middle_norm, grad_gain_two, grad_shift_two = norm_two_pull(grad_normed_two)
    grad_middle = grad_out + grad_middle_norm
    grad_branch = (gain_all[1] * grad_middle).astype(jnp.bfloat16)
    grad_gain_one = jnp.sum(grad_middle * branch, axis=0)
    grad_bias_proj = jnp.sum(grad_branch.astype(jnp.float32), axis=0)
    grad_proj = jnp.einsum(
        "rd,re->de", attended, grad_branch, preferred_element_type=jnp.float32
    ).astype(jnp.bfloat16)
    grad_proj, grad_branch = lax.optimization_barrier((grad_proj, grad_branch))
    grad_attended = jnp.einsum("re,de->rd", grad_branch, w_proj, preferred_element_type=jnp.float32)
    grad_attended = grad_attended.astype(jnp.bfloat16)
    grad_attended, sum_down, grad_up = lax.optimization_barrier((grad_attended, sum_down, grad_up))
    sum_up = reduce_rows(grad_up)
    grad_query_round, grad_key_all, grad_value_all = attend_back(
        queries, key_all, value_all, grad_attended, log_totals, key_valid
    )
    grad_key_all, grad_value_all, sum_up, grad_proj = lax.optimization_barrier(
        (grad_key_all, grad_value_all, sum_up, grad_proj)
    )
    sum_proj = reduce_rows(grad_proj)
    grad_keys = scatter_rows(grad_key_all)
    grad_values = scatter_rows(grad_value_all)
    grad_queries = (grad_query_round.astype(jnp.float32) * query_scale).astype(jnp.bfloat16)
    grad_mixed = jnp.concatenate([grad_queries, grad_keys, grad_values], axis=1)
    grad_bias_query = jnp.sum(grad_queries.astype(jnp.float32), axis=0)
    grad_bias_value = jnp.sum(grad_values.astype(jnp.float32), axis=0)
    grad_qkv = jnp.einsum(
        "rd,re->de", normed, grad_mixed, preferred_element_type=jnp.float32
    ).astype(jnp.bfloat16)
    grad_qkv, grad_mixed, sum_proj = lax.optimization_barrier((grad_qkv, grad_mixed, sum_proj))
    sum_qkv = reduce_rows(grad_qkv)
    grad_normed = jnp.einsum("re,de->rd", grad_mixed, w_qkv, preferred_element_type=jnp.float32)
    _, norm_one_pull = jax.vjp(norm_rows, values, gain_all[0], bias_all[0])
    grad_values_norm, grad_gain_zero, grad_shift_zero = norm_one_pull(grad_normed)
    input_grad = (
        give_rows(((grad_middle + grad_values_norm) * row_valid).astype(jnp.bfloat16))[None]
    )
    grad_gains = jnp.stack([grad_gain_zero, grad_gain_one, grad_gain_two, grad_gain_three])
    grad_biases = jnp.concatenate(
        [
            jnp.stack(
                [
                    grad_shift_zero,
                    grad_bias_query,
                    grad_bias_value,
                    grad_bias_proj,
                    grad_shift_two,
                    grad_bias_down,
                ]
            ),
            grad_bias_up,
        ],
        axis=0,
    )
    grad_rows, sum_qkv = lax.optimization_barrier(
        (jnp.concatenate([grad_gains, grad_biases], axis=0), sum_qkv)
    )
    small = lax.psum_scatter(
        grad_rows,
        ("img", "tok"),
        scatter_dimension=1,
        tiled=True,
    )
    summed = (
        sum_qkv,
        sum_proj,
        sum_up,
        sum_down,
        small[:gain_count],
        small[gain_count:],
    )
    params = (qkv_weight, proj_weight, up_weight, down_weight, gain_rows, bias_rows)
    firsts = (qkv_first, proj_first, up_first, down_first, gain_first, bias_first)
    seconds = (qkv_second, proj_second, up_second, down_second, gain_second, bias_second)
    updated = [
        adam_update(
            params[position],
            summed[position],
            firsts[position],
            seconds[position],
            learn_rates[position],
            decay_rates[position],
        )
        for position in range(6)
    ]
    return (
        output,
        input_grad,
        updated[0][0],
        updated[1][0],
        updated[2][0],
        updated[3][0],
        updated[4][0],
        updated[5][0],
        updated[0][1],
        updated[1][1],
        updated[2][1],
        updated[3][1],
        updated[4][1],
        updated[5][1],
        updated[0][2],
        updated[1][2],
        updated[2][2],
        updated[3][2],
        updated[4][2],
        updated[5][2],
    )


def solution(mesh):
    return jax.shard_map(
        per_device,
        mesh=mesh,
        in_specs=(
            P("img", "tok", None),
            P("img", None),
            P("img", "tok", None),
            P(("img", "tok"), None),
            P(("img", "tok"), None),
            P(("img", "tok"), None),
            P(("img", "tok"), None),
            P(None, ("img", "tok")),
            P(None, ("img", "tok")),
            P(("img", "tok"), None),
            P(("img", "tok"), None),
            P(("img", "tok"), None),
            P(("img", "tok"), None),
            P(None, ("img", "tok")),
            P(None, ("img", "tok")),
            P(("img", "tok"), None),
            P(("img", "tok"), None),
            P(("img", "tok"), None),
            P(("img", "tok"), None),
            P(None, ("img", "tok")),
            P(None, ("img", "tok")),
        ),
        out_specs=(
            P("img", "tok", None),
            P("img", "tok", None),
            P(("img", "tok"), None),
            P(("img", "tok"), None),
            P(("img", "tok"), None),
            P(("img", "tok"), None),
            P(None, ("img", "tok")),
            P(None, ("img", "tok")),
            P(("img", "tok"), None),
            P(("img", "tok"), None),
            P(("img", "tok"), None),
            P(("img", "tok"), None),
            P(None, ("img", "tok")),
            P(None, ("img", "tok")),
            P(("img", "tok"), None),
            P(("img", "tok"), None),
            P(("img", "tok"), None),
            P(("img", "tok"), None),
            P(None, ("img", "tok")),
            P(None, ("img", "tok")),
        ),
        check_vma=False,
    )
```
